32 devices in a mesh: pole: 2 (over y), prow: 1, pcol: 16 (over z, x, core).
Axes of the slice: x: 2, y: 2, z: 4, core: 2. Of those that a mesh axis runs over, the one named last changes fastest.
Arguments:
- anc_inverse: float32 [12288, 6144], P(('pole', 'prow'), 'pcol'), parts along dimension 0, may hold values from -8 to 8
- anc_factor: float32 [12288, 768], P(('pole', 'pcol')), parts along dimension 0, may hold values from -0.078125 to 0.078125
- win_factor: float32 [1536, 768], P('pole'), parts along dimension 0, may hold values from -0.375 to 0.375
- pivot_inverse: float32 [6, 256, 256], P('pole'), parts along dimension 0, may hold values from -6 to 6
- structure: int32 [3, 24], replicated, may hold values 0 or 1
Outputs:
- anc_columns: float32 [12288, 768], P(('pole', 'prow', 'pcol')), parts along dimension 0
- win_inverse: float32 [1536, 768], P('pole'), parts along dimension 0
The draws below stay inside these ranges and needn't reach their ends.
There are 2 independent parts, one for each index of `pole`. The reference program is written for one: setup_inputs(seed, part) draws one part's arguments, and reference() takes and returns one part's arrays. A program takes and returns all parts, laid end to end along the dimension named above; an argument that names none is the same for every part. Nothing has to cross between parts.
All inputs are finite; a program needn't handle non-finite values.
Results may differ from the reference program's by a relative error of at most 0.0001.
Values sent between devices are 32-bit elements; how exact they have to be, the bound alone decides.
A program may use at most 128 MiB of HBM per device.

```python
import jax
import jax.numpy as jnp
from jax import lax

W = 256
STEPS = 3
NA = 6144
NAB = 24
SW = 768


def draw_anc_inverse(key, part):
    entry_key = jax.random.fold_in(jax.random.fold_in(key, 11), 0)
    entries = jnp.clip(jax.random.normal(entry_key, (NA, NA), jnp.float32), -5.0, 5.0)
    return (entries + entries.T) * 0.7071


def plant(values, key, low, high):
    index_at = [jax.random.randint(jax.random.fold_in(key, axis), (), 0, length) for axis, length in enumerate(values.shape)]
    widest = values.shape.index(max(values.shape))
    next_to = index_at[:widest] + [(index_at[widest] + 1) % values.shape[widest]] + index_at[widest + 1:]
    return values.at[tuple(index_at)].set(low).at[tuple(next_to)].set(high)


def steps_of(stream_key, dims, cuts, least, high):
    gain = 1.0
    for axis_at, shards_of in cuts:
        heights = jax.random.uniform(jax.random.fold_in(jax.random.fold_in(stream_key, 6), axis_at), (shards_of,), jnp.float32, least / len(cuts), high / len(cuts))
        gain = gain * jnp.repeat(jnp.exp(heights), dims[axis_at] // shards_of).reshape((-1,) + (1,) * (len(dims) - 1 - axis_at))
    return gain


def scatter_about(rng, shape, deviation, reach, cuts=(), kind=jnp.bfloat16):
    array = deviation * jax.random.normal(rng, shape, jnp.float32)
    if cuts:
        array = array * steps_of(rng, shape, cuts, -0.22, 0.18)
    return jnp.clip(array, -reach, reach).astype(kind)


def setup_inputs(seed: int = 0, part: int = 0) -> dict:
    arg_keys = jax.random.split(jax.random.key(seed), 6)
    part_keys = jax.random.split(jax.random.fold_in(arg_keys[5], part), 6)
    anc_inverse = draw_anc_inverse(jax.random.fold_in(jax.random.fold_in(arg_keys[5], part), 71), part)
    anc_factor = scatter_about(part_keys[1], (NA, SW), NA ** -0.5, 0.078125, ((0, 16),), jnp.float32)
    win_factor = scatter_about(part_keys[2], (SW, SW), W ** -0.5, 0.375, (), jnp.float32)
    pivot_inverse = scatter_about(part_keys[3], (STEPS, W, W), 1.0, 6.0, (), jnp.float32)
    structure = plant((jax.random.randint(arg_keys[4], (STEPS, NAB), 0, 4) < 3).astype(jnp.int32), jax.random.fold_in(arg_keys[4], 1), 0, 1)
    return dict(anc_inverse=anc_inverse, anc_factor=anc_factor, win_factor=win_factor, pivot_inverse=pivot_inverse, structure=structure)


precise = lax.Precision.HIGHEST


def product(left, right):
    return jnp.dot(left, right, precision=precise, preferred_element_type=jnp.float32)


def reference(anc_inverse, anc_factor, win_factor, pivot_inverse, structure):
    row_block = (jnp.arange(NA) // W).astype(jnp.int32)
    kept_rows = jnp.take(structure, row_block, axis=1).astype(jnp.float32).T
    column_store = {}
    window_blocks = {}
    for k in range(STEPS - 1, -1, -1):
        first_col = k * W
        factor_now = anc_factor[:, first_col:first_col + W] * kept_rows[:, k:k + 1]
        product_term = product(anc_inverse, factor_now)
        finished = list(range(k + 1, STEPS))
        if finished:
            stacked = jnp.concatenate([column_store[j] for j in finished], axis=1)
            column_now = -(product_term + product(stacked, win_factor[first_col + W:, first_col:first_col + W]))
        else:
            column_now = -product_term
        for j in finished:
            running = product(column_store[j].T, factor_now)
            for i in finished:
                running = running + product(window_blocks[(j, i)], win_factor[i * W:(i + 1) * W, first_col:first_col + W])
            window_blocks[(j, k)] = -running
            window_blocks[(k, j)] = -running.T
        pivot_block = pivot_inverse[k] - product(factor_now.T, column_now)
        for j in finished:
            pivot_block = pivot_block - product(win_factor[j * W:(j + 1) * W, first_col:first_col + W].T, window_blocks[(j, k)])
        window_blocks[(k, k)] = pivot_block
        column_store[k] = column_now
    anc_columns = jnp.concatenate([column_store[k] for k in range(STEPS)], axis=1)
    win_inverse = jnp.concatenate([jnp.concatenate([window_blocks[(i, k)] for k in range(STEPS)], axis=1) for i in range(STEPS)], axis=0)
    return (anc_columns, win_inverse)
```

```python
import functools

import jax
import jax.numpy as jnp
from jax import lax
from jax.experimental import pallas as pl
from jax.experimental.pallas import tpu as pltpu
from jax.sharding import PartitionSpec as P

MESH = pl.DeviceIdType.MESH
UP, DOWN, ACROSS, MATE = range(4)
Z = 4
LANES = 8


def split(value):
    high = value.astype(jnp.bfloat16)
    low = (value - high.astype(jnp.float32)).astype(jnp.bfloat16)
    return high, low


def dot3(left, right):
    (lh, ll), (rh, rl) = left, right
    dot = functools.partial(jnp.dot, preferred_element_type=jnp.float32)
    return dot(lh, rh) + (dot(lh, rl) + dot(ll, rh))


def mul(left, right):
    return dot3(split(left), split(right))


def fused_kernel(steps, width, anc_ref, fac_ref, win_ref, piv_ref, str_ref, cols_ref, out_ref, *scratch):
    (gath, fac_st, anc_st, win_st, piv_st, tr_hi, tr_lo, acc, pivot_rest) = scratch[:9]
    parts = scratch[9 : 9 + steps]
    mates = scratch[9 + steps : 9 + 2 * steps]
    halves = scratch[9 + 2 * steps : 9 + 3 * steps]
    slots = scratch[9 + 3 * steps : 9 + 4 * steps]
    sums = scratch[9 + 4 * steps : 9 + 5 * steps]
    (load_sem, send_sem, recv_sem, s1, r1, s2, r2, s3, r3, s4, r4) = scratch[9 + 5 * steps :]

    me = lax.axis_index("pcol")
    core = lax.rem(me, 2)
    x = lax.rem(me // 2, 2)
    z = me // 4
    lane = me // 2
    rows = fac_st.shape[0]
    half = width // 2
    piece = half // LANES
    mate = me + 1 - 2 * core

    def index(zz, xx, cc):
        return (zz * 2 + xx) * 2 + cc

    across = index(z, 1 - x, core)

    load_fac = pltpu.make_async_copy(fac_ref, fac_st, load_sem.at[0])
    load_anc = pltpu.make_async_copy(anc_ref, anc_st, load_sem.at[1])
    load_win = pltpu.make_async_copy(win_ref, win_st, load_sem.at[2])
    load_piv = pltpu.make_async_copy(piv_ref, piv_st, load_sem.at[3])
    load_fac.start()

    barrier = pltpu.get_barrier_semaphore()
    for d in range(1, LANES):
        peer = lax.rem(lane + d, LANES) * 2 + core
        pl.semaphore_signal(barrier, inc=1, device_id={"pcol": peer}, device_id_type=MESH)
    pl.semaphore_signal(barrier, inc=1, device_id={"pcol": mate}, device_id_type=MESH)

    load_fac.wait()
    load_anc.start()
    load_win.start()
    load_piv.start()
    sub = width // 2

    def mask_own(k):
        for piece_at in range(rows // sub):
            block = (me * (rows // sub) + piece_at) // 2
            kept = str_ref[k, block].astype(jnp.float32)
            gath[k, me, piece_at * sub : (piece_at + 1) * sub, :] = (
                fac_st[piece_at * sub : (piece_at + 1) * sub, k * width : (k + 1) * width] * kept
            )

    mask_own(steps - 1)
    pl.semaphore_wait(barrier, LANES)

    def remote(kind, k, block, dest):
        return pltpu.make_async_remote_copy(
            src_ref=gath.at[k, block],
            dst_ref=gath.at[k, block],
            send_sem=send_sem.at[kind, k, block],
            recv_sem=recv_sem.at[k, block],
            device_id={"pcol": dest},
            device_id_type=MESH,
        )

    def order(t):
        inner = (0, 0, 2, 3) if t else (1, 1, 1, 1)
        lowmid = inner[t] if t else 1
        highmid = 3 - lowmid
        return jnp.where(z == 0, t, jnp.where(z == 1, lowmid, jnp.where(z == 2, highmid, 3 - t)))

    def column_sends(k, t, act):
        zz = order(t)
        block = index(zz, x, core)

        def vertical(kind, dest, cond):
            @pl.when(cond)
            def _():
                act(remote(kind, k, block, dest))

        if t == 0:
            vertical(UP, jnp.minimum(me + 4, 4 * Z - 1), z < Z - 1)
            vertical(DOWN, jnp.maximum(me - 4, 0), z > 0)
        else:
            vertical(UP, jnp.minimum(me + 4, 4 * Z - 1), (zz < z) & (z < Z - 1))
            vertical(DOWN, jnp.maximum(me - 4, 0), (zz > z) & (z > 0))
        act(remote(ACROSS, k, block, across))
        act(remote(MATE, k, block, mate))

    def arrived(k, block):
        remote(MATE, k, block, mate).wait_recv()

    def column_event(k, t):
        if t > 0:
            arrived(k, index(order(t), x, core))
        column_sends(k, t, lambda copy: copy.start())

    def across_event(k, t):
        block = index(order(t), 1 - x, core)
        arrived(k, block)
        remote(MATE, k, block, mate).start()

    def compute_event(k, t):
        zz = order(t)
        arrived(k, index(zz, x, 1 - core))
        arrived(k, index(zz, 1 - x, 1 - core))

        def body(i, carry):
            block = zz * 4 + i
            if k == steps - 1:
                tile = anc_st[pl.ds(pl.multiple_of(block * rows, rows), rows), :].T
                high, low = split(tile)
                tr_hi[block] = high
                tr_lo[block] = low
            else:
                high, low = tr_hi[block], tr_lo[block]
            term = dot3((high, low), split(gath[k, block]))
            acc[...] += term
            return carry

        if t == 0:
            acc[...] = jnp.zeros_like(acc)
        lax.fori_loop(0, 4, body, 0)

    def fac_block(j, k):
        return win_st[j * width : (j + 1) * width, k * width : (k + 1) * width]

    def finish(k):
        total = acc[...]
        for j in range(k + 1, steps):
            total = total + mul(cols_ref[:, j * width : (j + 1) * width], fac_block(j, k))
        column = -total
        cols_ref[:, k * width : (k + 1) * width] = column
        flipped = split(column.T)
        for i in range(k + 1):
            parts[k][:, i * width : (i + 1) * width] = dot3(flipped, split(gath[i, me]))

    def mate_copy(k):
        return pltpu.make_async_remote_copy(
            src_ref=parts[k].at[pl.ds(pl.multiple_of((1 - core) * half, half), half), :],
            dst_ref=mates[k],
            send_sem=s1.at[k],
            recv_sem=r1.at[k],
            device_id={"pcol": mate},
            device_id_type=MESH,
        )

    def scatter_copy(k, d):
        peer = lax.rem(lane + d, LANES)
        return pltpu.make_async_remote_copy(
            src_ref=halves[k].at[pl.ds(pl.multiple_of(peer * piece, piece), piece), :],
            dst_ref=slots[k].at[lane],
            send_sem=s2.at[k, peer],
            recv_sem=r2.at[k, lane],
            device_id={"pcol": peer * 2 + core},
            device_id_type=MESH,
        )

    def scatter_wait(k, d):
        peer = lax.rem(lane + d, LANES)
        pltpu.make_async_remote_copy(
            src_ref=slots[k].at[peer],
            dst_ref=slots[k].at[peer],
            send_sem=s2.at[k, peer],
            recv_sem=r2.at[k, peer],
            device_id={"pcol": peer * 2 + core},
            device_id_type=MESH,
        ).wait_recv()

    def spread_copy(k, d, owner):
        peer = lax.rem(lane + d, LANES)
        at = pl.ds(pl.multiple_of(core * half + owner * piece, piece), piece)
        return pltpu.make_async_remote_copy(
            src_ref=sums[k].at[at, :],
            dst_ref=sums[k].at[at, :],
            send_sem=s3.at[k, peer],
            recv_sem=r3.at[k, owner],
            device_id={"pcol": peer * 2 + core},
            device_id_type=MESH,
        )

    def join_copy(k, which):
        at = pl.ds(pl.multiple_of(which * half, half), half)
        return pltpu.make_async_remote_copy(
            src_ref=sums[k].at[at, :],
            dst_ref=sums[k].at[at, :],
            send_sem=s4.at[k],
            recv_sem=r4.at[k],
            device_id={"pcol": mate},
            device_id_type=MESH,
        )

    def phase(k, number):
        if number == 1:
            mate_copy(k).start()
        elif number == 2:
            mate_copy(k).wait_recv()
            own = pl.ds(pl.multiple_of(core * half, half), half)
            halves[k][...] = parts[k][own, :] + mates[k][...]
            for d in range(1, LANES):
                scatter_copy(k, d).start()
        elif number == 3:
            total = halves[k][pl.ds(pl.multiple_of(lane * piece, piece), piece), :]
            for d in range(1, LANES):
                scatter_wait(k, d)
                total = total + slots[k][lax.rem(lane + d, LANES)]
            sums[k][pl.ds(pl.multiple_of(core * half + lane * piece, piece), piece), :] = total
            for d in range(1, LANES):
                spread_copy(k, d, lane).start()
        elif number == 4:
            for d in range(1, LANES):
                spread_copy(k, d, lax.rem(lane + d, LANES)).wait_recv()
            join_copy(k, core).start()
        else:
            join_copy(k, 1 - core).wait_recv()
            window(k)

    def put(j, k, value):
        out_ref[j * width : (j + 1) * width, k * width : (k + 1) * width] = value

    def got(j, k):
        return out_ref[j * width : (j + 1) * width, k * width : (k + 1) * width]

    def summed(j, k):
        return sums[j][:, k * width : (k + 1) * width]

    def window(k):
        if k == 0:
            put(0, 0, pivot_rest[...] - summed(0, 0).T)
            return
        diag = piv_st[k] - summed(k, k).T
        for j in range(k + 1, steps):
            diag = diag - mul(fac_block(j, k).T, got(j, k))
        put(k, k, diag)
        low = k - 1
        for j in range(k, steps):
            running = summed(j, low)
            for i in range(k, steps):
                running = running + mul(got(j, i), fac_block(i, low))
            put(j, low, -running)
            put(low, j, -running.T)
        if low == 0:
            rest = piv_st[0]
            for j in range(1, steps):
                rest = rest - mul(fac_block(j, 0).T, got(j, 0))
            pivot_rest[...] = rest

    events = [(k, t) for k in range(steps - 1, -1, -1) for t in range(Z)]
    lag_across, lag_compute = 1, 2
    pending = []
    for g in range(len(events) + lag_compute):
        if g < len(events):
            column_event(*events[g])
        if g == 0:
            for k in range(steps - 1):
                mask_own(k)
            load_anc.wait()
            load_win.wait()
            load_piv.wait()
        if 0 <= g - lag_across < len(events):
            across_event(*events[g - lag_across])
        for k, first in pending:
            number = g - first + 1
            if 2 <= number <= 5:
                phase(k, number)
        if g >= lag_compute:
            k, t = events[g - lag_compute]
            compute_event(k, t)
            if t == Z - 1:
                finish(k)
                phase(k, 1)
                pending.append((k, g))
    for g in range(len(events) + lag_compute, len(events) + lag_compute + 4):
        for k, first in pending:
            number = g - first + 1
            if 2 <= number <= 5:
                phase(k, number)

    for k, t in events:
        column_sends(k, t, lambda copy: copy.wait_send())
        remote(MATE, k, index(order(t), 1 - x, core), mate).wait_send()
    for k in range(steps):
        mate_copy(k).wait_send()
        for d in range(1, LANES):
            scatter_copy(k, d).wait_send()
            spread_copy(k, d, lane).wait_send()
        join_copy(k, core).wait_send()


def fused(anc_inverse, anc_factor, win_factor, pivot_inverse, structure):
    steps, width = pivot_inverse.shape[:2]
    rows, all_cols = anc_factor.shape
    devices = lax.axis_size("pcol")
    half = width // 2
    piece = half // LANES
    f32, b16 = jnp.float32, jnp.bfloat16
    wide = [(k + 1) * width for k in range(steps)]
    dma = pltpu.SemaphoreType.DMA
    scratch = [
        pltpu.VMEM((steps, devices, rows, width), f32),
        pltpu.VMEM((rows, all_cols), f32),
        pltpu.VMEM(anc_inverse.shape, f32),
        pltpu.VMEM(win_factor.shape, f32),
        pltpu.VMEM(pivot_inverse.shape, f32),
        pltpu.VMEM((devices, rows, rows), b16),
        pltpu.VMEM((devices, rows, rows), b16),
        pltpu.VMEM((rows, width), f32),
        pltpu.VMEM((width, width), f32),
        *[pltpu.VMEM((width, w), f32) for w in wide],
        *[pltpu.VMEM((half, w), f32) for w in wide],
        *[pltpu.VMEM((half, w), f32) for w in wide],
        *[pltpu.VMEM((LANES, piece, w), f32) for w in wide],
        *[pltpu.VMEM((width, w), f32) for w in wide],
        dma((4,)),
        dma((4, steps, devices)),
        dma((steps, devices)),
        dma((steps,)),
        dma((steps,)),
        dma((steps, LANES)),
        dma((steps, LANES)),
        dma((steps, LANES)),
        dma((steps, LANES)),
        dma((steps,)),
        dma((steps,)),
    ]
    whole = pl.BlockSpec(memory_space=pl.ANY)
    vmem = pl.BlockSpec(memory_space=pltpu.VMEM)
    return pl.pallas_call(
        functools.partial(fused_kernel, steps, width),
        out_shape=(
            jax.ShapeDtypeStruct((rows, all_cols), f32),
            jax.ShapeDtypeStruct((all_cols, all_cols), f32),
        ),
        in_specs=[whole, whole, whole, whole, pl.BlockSpec(memory_space=pltpu.SMEM)],
        out_specs=(vmem, vmem),
        scratch_shapes=scratch,
        compiler_params=pltpu.CompilerParams(
            collective_id=0, has_side_effects=True, vmem_limit_bytes=62 * 2**20
        ),
    )(anc_inverse, anc_factor, win_factor, pivot_inverse, structure)


precise = lax.Precision.HIGHEST


def product(left, right):
    return jnp.dot(left, right, precision=precise, preferred_element_type=jnp.float32)


def on_device(anc_inverse, anc_factor, win_factor, pivot_inverse, structure):
    row_count = lax.axis_size("prow")
    col_count = lax.axis_size("pcol")
    if row_count == 1 and col_count == 4 * Z and 2 * anc_factor.shape[0] == 3 * pivot_inverse.shape[1]:
        return fused(anc_inverse, anc_factor, win_factor, pivot_inverse, structure)
    row_index = lax.axis_index("prow")
    col_index = lax.axis_index("pcol")
    block_rows = anc_inverse.shape[0]
    block_cols = anc_inverse.shape[1]
    steps_total = pivot_inverse.shape[0]
    width = pivot_inverse.shape[1]
    all_cols = anc_factor.shape[1]
    block_count = structure.shape[1]
    ratio_cols = col_count // row_count
    share_rows = block_rows // col_count
    structure_cols = structure.T.astype(jnp.float32)
    global_rows = col_index * block_cols + lax.iota(jnp.int32, block_cols)
    onehot_rows = (
        (global_rows // width)[:, None] == lax.iota(jnp.int32, block_count)[None, :]
    ).astype(jnp.float32)
    kept_rows = product(onehot_rows, structure_cols)
    share_offset = col_index * share_rows
    share_global = (row_index * col_count + col_index) * share_rows + lax.iota(
        jnp.int32, share_rows
    )
    onehot_share = (
        (share_global // width)[:, None] == lax.iota(jnp.int32, block_count)[None, :]
    ).astype(jnp.float32)
    kept_share = product(onehot_share, structure_cols)
    slot_ids = lax.iota(jnp.int32, col_count)
    source_flag = (slot_ids // row_count == col_index - row_index * ratio_cols).astype(jnp.float32)
    pieces = jnp.tile(anc_factor.reshape(row_count, share_rows, all_cols), (ratio_cols, 1, 1))
    outgoing = pieces * source_flag[:, None, None]
    incoming = lax.all_to_all(outgoing, "pcol", split_axis=0, concat_axis=0, tiled=True)
    factor_share = jnp.sum(incoming, axis=0)
    column_store = {}
    share_store = {}
    window_blocks = {}
    for k in range(steps_total - 1, -1, -1):
        first_col = k * width
        factor_now = anc_factor[:, first_col : first_col + width] * kept_rows[:, k : k + 1]
        share_factor = factor_share[:, first_col : first_col + width] * kept_share[:, k : k + 1]
        finished = list(range(k + 1, steps_total))
        if finished:
            stacked = jnp.concatenate([column_store[j] for j in finished], axis=1)
            factor_win = win_factor[first_col + width :, first_col : first_col + width]

        def term_rows(start, count, factor_now=factor_now):
            return product(anc_inverse, factor_now)

        share_image = lax.psum_scatter(
            term_rows(jnp.int32(0), share_rows * lax.axis_size("pcol")),
            "pcol",
            scatter_dimension=0,
            tiled=True,
        )
        if finished:
            share_image = share_image + product(
                lax.dynamic_slice_in_dim(stacked, share_offset, share_rows, 0), factor_win
            )
        share_column = -share_image
        column_now = lax.all_gather(share_column, "pcol", axis=0, tiled=True)
        crossings = [product(share_store[j].T, share_factor) for j in finished]
        pivot_part = product(share_factor.T, share_column)
        cross_sums = []
        if finished:
            cross_total = lax.psum(jnp.stack(crossings), ("prow", "pcol"))
            cross_sums = [cross_total[position] for position in range(len(finished))]
        pivot_sum = lax.psum(pivot_part, ("prow", "pcol"))
        for position, j in enumerate(finished):
            running = cross_sums[position]
            for i in finished:
                running = running + product(
                    window_blocks[j, i],
                    win_factor[i * width : (i + 1) * width, first_col : first_col + width],
                )
            window_blocks[j, k] = -running
            window_blocks[k, j] = -running.T
        pivot_block = pivot_inverse[k] - pivot_sum
        for j in finished:
            pivot_block = pivot_block - product(
                win_factor[j * width : (j + 1) * width, first_col : first_col + width].T,
                window_blocks[j, k],
            )
        window_blocks[k, k] = pivot_block
        column_store[k] = column_now
        share_store[k] = share_column
    anc_columns = jnp.concatenate([share_store[k] for k in range(steps_total)], axis=1)
    win_inverse = jnp.concatenate(
        [
            jnp.concatenate([window_blocks[i, k] for k in range(steps_total)], axis=1)
            for i in range(steps_total)
        ],
        axis=0,
    )
    return (anc_columns, win_inverse)


def solution(mesh):
    in_specs = (
        P(("pole", "prow"), "pcol"),
        P(("pole", "pcol"), None),
        P("pole", None),
        P("pole", None, None),
        P(),
    )
    out_specs = (P(("pole", "prow", "pcol"), None), P("pole", None))
    return jax.shard_map(
        on_device, mesh=mesh, in_specs=in_specs, out_specs=out_specs, check_vma=False
    )
```

```python
import functools

import jax
import jax.numpy as jnp
from jax import lax
from jax.experimental import pallas as pl
from jax.experimental.pallas import tpu as pltpu
from jax.sharding import PartitionSpec as P

MESH = pl.DeviceIdType.MESH
UP, DOWN, ACROSS, MATE = range(4)
Z = 4
LANES = 8


def split(value):
    high = value.astype(jnp.bfloat16)
    low = (value - high.astype(jnp.float32)).astype(jnp.bfloat16)
    return high, low


def dot3(left, right):
    (lh, ll), (rh, rl) = left, right
    dot = functools.partial(jnp.dot, preferred_element_type=jnp.float32)
    return dot(lh, rh) + (dot(lh, rl) + dot(ll, rh))


def mul(left, right):
    return dot3(split(left), split(right))


def fused_kernel(steps, width, anc_ref, fac_ref, win_ref, piv_ref, str_ref, cols_ref, out_ref, *scratch):
    (gath, fac_st, anc_st, win_st, piv_st, tr_hi, tr_lo, acc, pivot_rest) = scratch[:9]
    parts = scratch[9 : 9 + steps]
    mates = scratch[9 + steps : 9 + 2 * steps]
    halves = scratch[9 + 2 * steps : 9 + 3 * steps]
    slots = scratch[9 + 3 * steps : 9 + 4 * steps]
    sums = scratch[9 + 4 * steps : 9 + 5 * steps]
    (load_sem, send_sem, recv_sem, s1, r1, s2, r2, s3, r3, s4, r4) = scratch[9 + 5 * steps :]

    me = lax.axis_index("pcol")
    core = lax.rem(me, 2)
    x = lax.rem(me // 2, 2)
    z = me // 4
    lane = me // 2
    rows = fac_st.shape[0]
    half = width // 2
    piece = half // LANES
    mate = me + 1 - 2 * core

    def index(zz, xx, cc):
        return (zz * 2 + xx) * 2 + cc

    across = index(z, 1 - x, core)

    load_fac = pltpu.make_async_copy(fac_ref, fac_st, load_sem.at[0])
    load_anc = pltpu.make_async_copy(anc_ref, anc_st, load_sem.at[1])
    load_win = pltpu.make_async_copy(win_ref, win_st, load_sem.at[2])
    load_piv = pltpu.make_async_copy(piv_ref, piv_st, load_sem.at[3])
    load_fac.start()

    barrier = pltpu.get_barrier_semaphore()
    for d in range(1, LANES):
        peer = lax.rem(lane + d, LANES) * 2 + core
        pl.semaphore_signal(barrier, inc=1, device_id={"pcol": peer}, device_id_type=MESH)
    pl.semaphore_signal(barrier, inc=1, device_id={"pcol": mate}, device_id_type=MESH)

    load_fac.wait()
    load_anc.start()
    load_win.start()
    load_piv.start()
    sub = width // 2

    def mask_own(k):
        for piece_at in range(rows // sub):
            block = (me * (rows // sub) + piece_at) // 2
            kept = str_ref[k, block].astype(jnp.float32)
            gath[k, me, piece_at * sub : (piece_at + 1) * sub, :] = (
                fac_st[piece_at * sub : (piece_at + 1) * sub, k * width : (k + 1) * width] * kept
            )

    mask_own(steps - 1)
    pl.semaphore_wait(barrier, LANES)

    def remote(kind, k, block, dest):
        return pltpu.make_async_remote_copy(
            src_ref=gath.at[k, block],
            dst_ref=gath.at[k, block],
            send_sem=send_sem.at[kind, k, block],
            recv_sem=recv_sem.at[k, block],
            device_id={"pcol": dest},
            device_id_type=MESH,
        )

    def order(t):
        inner = (0, 0, 2, 3) if t else (1, 1, 1, 1)
        lowmid = inner[t] if t else 1
        highmid = 3 - lowmid
        return jnp.where(z == 0, t, jnp.where(z == 1, lowmid, jnp.where(z == 2, highmid, 3 - t)))

    def column_sends(k, t, act):
        zz = order(t)
        block = index(zz, x, core)

        def vertical(kind, dest, cond):
            @pl.when(cond)
            def _():
                act(remote(kind, k, block, dest))

        if t == 0:
            vertical(UP, jnp.minimum(me + 4, 4 * Z - 1), z < Z - 1)
            vertical(DOWN, jnp.maximum(me - 4, 0), z > 0)
        else:
            vertical(UP, jnp.minimum(me + 4, 4 * Z - 1), (zz < z) & (z < Z - 1))
            vertical(DOWN, jnp.maximum(me - 4, 0), (zz > z) & (z > 0))
        act(remote(ACROSS, k, block, across))
        act(remote(MATE, k, block, mate))

    def arrived(k, block):
        remote(MATE, k, block, mate).wait_recv()

    def column_event(k, t):
        if t > 0:
            arrived(k, index(order(t), x, core))
        column_sends(k, t, lambda copy: copy.start())

    def across_event(k, t):
        block = index(order(t), 1 - x, core)
        arrived(k, block)
        remote(MATE, k, block, mate).start()

    def compute_event(k, t):
        zz = order(t)
        arrived(k, index(zz, x, 1 - core))
        arrived(k, index(zz, 1 - x, 1 - core))

        def body(i, carry):
            block = zz * 4 + i
            if k == steps - 1:
                tile = anc_st[pl.ds(pl.multiple_of(block * rows, rows), rows), :].T
                high, low = split(tile)
                tr_hi[block] = high
                tr_lo[block] = low
            else:
                high, low = tr_hi[block], tr_lo[block]
            term = dot3((high, low), split(gath[k, block]))
            acc[...] += term
            return carry

        if t == 0:
            start = jnp.zeros(acc.shape, jnp.float32)
            for j in range(k + 1, steps):
                start = start + mul(cols_ref[:, j * width : (j + 1) * width], fac_block(j, k))
            acc[...] = start
        lax.fori_loop(0, 4, body, 0)

    def fac_block(j, k):
        return win_st[j * width : (j + 1) * width, k * width : (k + 1) * width]

    def finish(k):
        column = -acc[...]
        cols_ref[:, k * width : (k + 1) * width] = column
        flipped = split(column.T)
        for i in range(k + 1):
            parts[k][:, i * width : (i + 1) * width] = dot3(flipped, split(gath[i, me]))

    def mate_copy(k):
        return pltpu.make_async_remote_copy(
            src_ref=parts[k].at[pl.ds(pl.multiple_of((1 - core) * half, half), half), :],
            dst_ref=mates[k],
            send_sem=s1.at[k],
            recv_sem=r1.at[k],
            device_id={"pcol": mate},
            device_id_type=MESH,
        )

    def scatter_copy(k, d):
        peer = lax.rem(lane + d, LANES)
        return pltpu.make_async_remote_copy(
            src_ref=halves[k].at[pl.ds(pl.multiple_of(peer * piece, piece), piece), :],
            dst_ref=slots[k].at[lane],
            send_sem=s2.at[k, peer],
            recv_sem=r2.at[k, lane],
            device_id={"pcol": peer * 2 + core},
            device_id_type=MESH,
        )

    def scatter_wait(k, d):
        peer = lax.rem(lane + d, LANES)
        pltpu.make_async_remote_copy(
            src_ref=slots[k].at[peer],
            dst_ref=slots[k].at[peer],
            send_sem=s2.at[k, peer],
            recv_sem=r2.at[k, peer],
            device_id={"pcol": peer * 2 + core},
            device_id_type=MESH,
        ).wait_recv()

    def spread_copy(k, d, owner):
        peer = lax.rem(lane + d, LANES)
        at = pl.ds(pl.multiple_of(core * half + owner * piece, piece), piece)
        return pltpu.make_async_remote_copy(
            src_ref=sums[k].at[at, :],
            dst_ref=sums[k].at[at, :],
            send_sem=s3.at[k, peer],
            recv_sem=r3.at[k, owner],
            device_id={"pcol": peer * 2 + core},
            device_id_type=MESH,
        )

    def join_copy(k, which):
        at = pl.ds(pl.multiple_of(which * half, half), half)
        return pltpu.make_async_remote_copy(
            src_ref=sums[k].at[at, :],
            dst_ref=sums[k].at[at, :],
            send_sem=s4.at[k],
            recv_sem=r4.at[k],
            device_id={"pcol": mate},
            device_id_type=MESH,
        )

    def phase(k, number):
        if number == 1:
            mate_copy(k).start()
        elif number == 2:
            mate_copy(k).wait_recv()
            own = pl.ds(pl.multiple_of(core * half, half), half)
            halves[k][...] = parts[k][own, :] + mates[k][...]
            for d in range(1, LANES):
                scatter_copy(k, d).start()
        elif number == 3:
            total = halves[k][pl.ds(pl.multiple_of(lane * piece, piece), piece), :]
            for d in range(1, LANES):
                scatter_wait(k, d)
                total = total + slots[k][lax.rem(lane + d, LANES)]
            sums[k][pl.ds(pl.multiple_of(core * half + lane * piece, piece), piece), :] = total
            for d in range(1, LANES):
                spread_copy(k, d, lane).start()
        elif number == 4:
            for d in range(1, LANES):
                spread_copy(k, d, lax.rem(lane + d, LANES)).wait_recv()
            join_copy(k, core).start()
        else:
            join_copy(k, 1 - core).wait_recv()
            window(k)

    def put(j, k, value):
        out_ref[j * width : (j + 1) * width, k * width : (k + 1) * width] = value

    def got(j, k):
        return out_ref[j * width : (j + 1) * width, k * width : (k + 1) * width]

    def summed(j, k):
        return sums[j][:, k * width : (k + 1) * width]

    def window(k):
        if k == 0:
            put(0, 0, pivot_rest[...] - summed(0, 0).T)
            return
        diag = piv_st[k] - summed(k, k).T
        for j in range(k + 1, steps):
            diag = diag - mul(fac_block(j, k).T, got(j, k))
        put(k, k, diag)
        low = k - 1
        for j in range(k, steps):
            running = summed(j, low)
            for i in range(k, steps):
                running = running + mul(got(j, i), fac_block(i, low))
            put(j, low, -running)
            put(low, j, -running.T)
        if low == 0:
            rest = piv_st[0]
            for j in range(1, steps):
                rest = rest - mul(fac_block(j, 0).T, got(j, 0))
            pivot_rest[...] = rest

    events = [(k, t) for k in range(steps - 1, -1, -1) for t in range(Z)]
    lag_across, lag_compute = 1, 2
    pending = []
    for g in range(len(events) + lag_compute):
        if g < len(events):
            column_event(*events[g])
        if g == 0:
            for k in range(steps - 1):
                mask_own(k)
            load_anc.wait()
            load_win.wait()
            load_piv.wait()
        if 0 <= g - lag_across < len(events):
            across_event(*events[g - lag_across])
        for k, first in pending:
            number = g - first + 1
            if 2 <= number <= (5 if k > 1 else 4):
                phase(k, number)
        if g >= lag_compute:
            k, t = events[g - lag_compute]
            compute_event(k, t)
            if t == Z - 1:
                finish(k)
                phase(k, 1)
                pending.append((k, g))
    phase(0, 2)
    phase(1, 5)
    for number in range(3, 6):
        phase(0, number)

    for k, t in events:
        column_sends(k, t, lambda copy: copy.wait_send())
        remote(MATE, k, index(order(t), 1 - x, core), mate).wait_send()
    for k in range(steps):
        mate_copy(k).wait_send()
        for d in range(1, LANES):
            scatter_copy(k, d).wait_send()
            spread_copy(k, d, lane).wait_send()
        join_copy(k, core).wait_send()


def fused(anc_inverse, anc_factor, win_factor, pivot_inverse, structure):
    steps, width = pivot_inverse.shape[:2]
    rows, all_cols = anc_factor.shape
    devices = lax.axis_size("pcol")
    half = width // 2
    piece = half // LANES
    f32, b16 = jnp.float32, jnp.bfloat16
    wide = [(k + 1) * width for k in range(steps)]
    dma = pltpu.SemaphoreType.DMA
    scratch = [
        pltpu.VMEM((steps, devices, rows, width), f32),
        pltpu.VMEM((rows, all_cols), f32),
        pltpu.VMEM(anc_inverse.shape, f32),
        pltpu.VMEM(win_factor.shape, f32),
        pltpu.VMEM(pivot_inverse.shape, f32),
        pltpu.VMEM((devices, rows, rows), b16),
        pltpu.VMEM((devices, rows, rows), b16),
        pltpu.VMEM((rows, width), f32),
        pltpu.VMEM((width, width), f32),
        *[pltpu.VMEM((width, w), f32) for w in wide],
        *[pltpu.VMEM((half, w), f32) for w in wide],
        *[pltpu.VMEM((half, w), f32) for w in wide],
        *[pltpu.VMEM((LANES, piece, w), f32) for w in wide],
        *[pltpu.VMEM((width, w), f32) for w in wide],
        dma((4,)),
        dma((4, steps, devices)),
        dma((steps, devices)),
        dma((steps,)),
        dma((steps,)),
        dma((steps, LANES)),
        dma((steps, LANES)),
        dma((steps, LANES)),
        dma((steps, LANES)),
        dma((steps,)),
        dma((steps,)),
    ]
    whole = pl.BlockSpec(memory_space=pl.ANY)
    vmem = pl.BlockSpec(memory_space=pltpu.VMEM)
    return pl.pallas_call(
        functools.partial(fused_kernel, steps, width),
        out_shape=(
            jax.ShapeDtypeStruct((rows, all_cols), f32),
            jax.ShapeDtypeStruct((all_cols, all_cols), f32),
        ),
        in_specs=[whole, whole, whole, whole, pl.BlockSpec(memory_space=pltpu.SMEM)],
        out_specs=(vmem, vmem),
        scratch_shapes=scratch,
        compiler_params=pltpu.CompilerParams(
            collective_id=0, has_side_effects=True, vmem_limit_bytes=62 * 2**20
        ),
    )(anc_inverse, anc_factor, win_factor, pivot_inverse, structure)


precise = lax.Precision.HIGHEST


def product(left, right):
    return jnp.dot(left, right, precision=precise, preferred_element_type=jnp.float32)


def on_device(anc_inverse, anc_factor, win_factor, pivot_inverse, structure):
    row_count = lax.axis_size("prow")
    col_count = lax.axis_size("pcol")
    if row_count == 1 and col_count == 4 * Z and 2 * anc_factor.shape[0] == 3 * pivot_inverse.shape[1]:
        return fused(anc_inverse, anc_factor, win_factor, pivot_inverse, structure)
    row_index = lax.axis_index("prow")
    col_index = lax.axis_index("pcol")
    block_rows = anc_inverse.shape[0]
    block_cols = anc_inverse.shape[1]
    steps_total = pivot_inverse.shape[0]
    width = pivot_inverse.shape[1]
    all_cols = anc_factor.shape[1]
    block_count = structure.shape[1]
    ratio_cols = col_count // row_count
    share_rows = block_rows // col_count
    structure_cols = structure.T.astype(jnp.float32)
    global_rows = col_index * block_cols + lax.iota(jnp.int32, block_cols)
    onehot_rows = (
        (global_rows // width)[:, None] == lax.iota(jnp.int32, block_count)[None, :]
    ).astype(jnp.float32)
    kept_rows = product(onehot_rows, structure_cols)
    share_offset = col_index * share_rows
    share_global = (row_index * col_count + col_index) * share_rows + lax.iota(
        jnp.int32, share_rows
    )
    onehot_share = (
        (share_global // width)[:, None] == lax.iota(jnp.int32, block_count)[None, :]
    ).astype(jnp.float32)
    kept_share = product(onehot_share, structure_cols)
    slot_ids = lax.iota(jnp.int32, col_count)
    source_flag = (slot_ids // row_count == col_index - row_index * ratio_cols).astype(jnp.float32)
    pieces = jnp.tile(anc_factor.reshape(row_count, share_rows, all_cols), (ratio_cols, 1, 1))
    outgoing = pieces * source_flag[:, None, None]
    incoming = lax.all_to_all(outgoing, "pcol", split_axis=0, concat_axis=0, tiled=True)
    factor_share = jnp.sum(incoming, axis=0)
    column_store = {}
    share_store = {}
    window_blocks = {}
    for k in range(steps_total - 1, -1, -1):
        first_col = k * width
        factor_now = anc_factor[:, first_col : first_col + width] * kept_rows[:, k : k + 1]
        share_factor = factor_share[:, first_col : first_col + width] * kept_share[:, k : k + 1]
        finished = list(range(k + 1, steps_total))
        if finished:
            stacked = jnp.concatenate([column_store[j] for j in finished], axis=1)
            factor_win = win_factor[first_col + width :, first_col : first_col + width]

        def term_rows(start, count, factor_now=factor_now):
            return product(anc_inverse, factor_now)

        share_image = lax.psum_scatter(
            term_rows(jnp.int32(0), share_rows * lax.axis_size("pcol")),
            "pcol",
            scatter_dimension=0,
            tiled=True,
        )
        if finished:
            share_image = share_image + product(
                lax.dynamic_slice_in_dim(stacked, share_offset, share_rows, 0), factor_win
            )
        share_column = -share_image
        column_now = lax.all_gather(share_column, "pcol", axis=0, tiled=True)
        crossings = [product(share_store[j].T, share_factor) for j in finished]
        pivot_part = product(share_factor.T, share_column)
        cross_sums = []
        if finished:
            cross_total = lax.psum(jnp.stack(crossings), ("prow", "pcol"))
            cross_sums = [cross_total[position] for position in range(len(finished))]
        pivot_sum = lax.psum(pivot_part, ("prow", "pcol"))
        for position, j in enumerate(finished):
            running = cross_sums[position]
            for i in finished:
                running = running + product(
                    window_blocks[j, i],
                    win_factor[i * width : (i + 1) * width, first_col : first_col + width],
                )
            window_blocks[j, k] = -running
            window_blocks[k, j] = -running.T
        pivot_block = pivot_inverse[k] - pivot_sum
        for j in finished:
            pivot_block = pivot_block - product(
                win_factor[j * width : (j + 1) * width, first_col : first_col + width].T,
                window_blocks[j, k],
            )
        window_blocks[k, k] = pivot_block
        column_store[k] = column_now
        share_store[k] = share_column
    anc_columns = jnp.concatenate([share_store[k] for k in range(steps_total)], axis=1)
    win_inverse = jnp.concatenate(
        [
            jnp.concatenate([window_blocks[i, k] for k in range(steps_total)], axis=1)
            for i in range(steps_total)
        ],
        axis=0,
    )
    return (anc_columns, win_inverse)


def solution(mesh):
    in_specs = (
        P(("pole", "prow"), "pcol"),
        P(("pole", "pcol"), None),
        P("pole", None),
        P("pole", None, None),
        P(),
    )
    out_specs = (P(("pole", "prow", "pcol"), None), P("pole", None))
    return jax.shard_map(
        on_device, mesh=mesh, in_specs=in_specs, out_specs=out_specs, check_vma=False
    )
```
